32 devices in a mesh: grp: 2 (over y), tile: 16 (over z, x, core).
Axes of the slice: x: 2, y: 2, z: 4, core: 2. Of those that a mesh axis runs over, the one named last changes fastest.
Arguments:
- first_feat: bfloat16 [448, 128, 256], P(('grp', 'tile')), parts along dimension 0, may hold values from -4 to 4
- second_feat: bfloat16 [448, 128, 256], P(('grp', 'tile')), parts along dimension 0, may hold values from -4 to 4
- hidden_init: bfloat16 [448, 128, 256], P(('grp', 'tile')), parts along dimension 0, may hold values from -4 to 4
- cotangent: bfloat16 [448, 128, 256], P(('grp', 'tile')), parts along dimension 0, may hold values from -6 to 6
- search_list: int32 [448, 4], P(('grp', 'tile')), parts along dimension 0, may hold values from 1 to 222, as said below
- offsets: int32 [2, 448], P(None, ('grp', 'tile')), parts along dimension 1, may hold values from -1 to 1
- lengths: int32 [448], P(('grp', 'tile')), parts along dimension 0, may hold values from 1 to 4
- hid_weight: bfloat16 [256, 512], replicated, may hold values from -0.375 to 0.375
- in_weight: bfloat16 [256, 768], replicated, may hold values from -0.375 to 0.375
- cand_weight: bfloat16 [256, 256], replicated, may hold values from -0.375 to 0.375
- disp_weight: float32 [2, 768], replicated, may hold values from -1.5 to 1.5
- gate_bias: float32 [768], replicated, may hold values from -1 to 1
Outputs:
- hidden_state: float32 [448, 128, 256], P(('grp', 'tile')), parts along dimension 0
- flow: float32 [448, 2, 128], P(('grp', 'tile')), parts along dimension 0
- grad_second: float32 [448, 128, 256], P(('grp', 'tile')), parts along dimension 0
The draws below stay inside these ranges and needn't reach their ends.
There are 2 independent parts, one for each index of `grp`. The reference program is written for one: setup_inputs(seed, part) draws one part's arguments, and reference() takes and returns one part's arrays. A program takes and returns all parts, laid end to end along the dimension named above; an argument that names none is the same for every part. Nothing has to cross between parts.
Inputs may be any that keep to these rules, and one draw needn't show every extreme that they name: `search_list`: the 4 ids of a block are distinct, and each, plus any offset of that block, names a block whose row lies within one block row of the block's own row.
All inputs are finite; a program needn't handle non-finite values.
Results may differ from the reference program's by a relative error of at most 0.0073.
Values may be sent and summed in bfloat16 or wider, within the bound.
A program may use at most 128 MiB of HBM per device.

```python
import math
import jax
import jax.numpy as jnp
from jax import lax

C = 256
PH = 8
PW = 16
P_SIZE = 128
BW = 7
BLOCKS = 224
SLOTS = 4
ITERS = 2


def draw_first_feat(key, part):
    key = jax.random.fold_in(key, 11)
    base_key = jax.random.fold_in(key, 0)
    field = jnp.clip(jax.random.normal(base_key, (BLOCKS, P_SIZE, C), jnp.float32), -4.0, 4.0)
    return field.astype(jnp.bfloat16)


def draw_second_feat(key, part):
    key = jax.random.fold_in(key, 13)
    base_key = jax.random.fold_in(key, 0)
    field = jnp.clip(jax.random.normal(base_key, (BLOCKS, P_SIZE, C), jnp.float32), -4.0, 4.0)
    return field.astype(jnp.bfloat16)


def draw_search_list(key, part):
    key = jax.random.fold_in(key, 21)
    row_count = BLOCKS // BW
    global_ids = jnp.arange(BLOCKS, dtype=jnp.int32)
    block_row = global_ids // BW
    low_row = jnp.maximum(block_row - 1, 0)
    high_row = jnp.minimum(block_row + 1, row_count - 1)
    lowest = low_row * BW + 1
    highest = (high_row + 1) * BW - 2
    column = jnp.arange(3 * BW, dtype=jnp.int32)
    candidate = (block_row[:, None] - 1) * BW + column[None, :]
    usable = (candidate >= lowest[:, None]) & (candidate <= highest[:, None])
    ranking = jax.random.randint(key, (BLOCKS, 3 * BW), 0, 1 << 20) * 64 + column[None, :]
    ranking = jnp.where(usable, ranking, -1)
    picked_values, picked = lax.top_k(ranking, SLOTS)
    return jnp.take_along_axis(candidate, picked, axis=1).astype(jnp.int32)


def draw_lengths(key, part):
    key = jax.random.fold_in(key, 31)
    centre_key, length_key = jax.random.split(key)
    row_count = BLOCKS // BW
    global_ids = jnp.arange(BLOCKS, dtype=jnp.int32)
    centre = jax.random.randint(centre_key, (), 1, row_count - 1)
    storm = jnp.abs(global_ids // BW - centre) <= 1
    drawn_length = jax.random.randint(length_key, (BLOCKS,), 1, 3)
    drawn_length = jnp.where(global_ids % BW == 0, 1, drawn_length)
    return jnp.where(storm, SLOTS, drawn_length).astype(jnp.int32)


def plant(drawn, key, smallest, largest):
    extent = drawn.shape
    index_at = [jax.random.randint(jax.random.fold_in(key, axis), (), 0, extent[axis]) for axis in range(len(extent))]
    drawn = drawn.at[tuple(index_at)].set(smallest)
    longest = extent.index(max(extent))
    index_at[longest] = (index_at[longest] + 1) % extent[longest]
    return drawn.at[tuple(index_at)].set(largest)


def shard_levels(stream_key, extent, pieces, smallest, high):
    factor_of, own = 1.0, jax.random.fold_in(stream_key, 6)
    for dim, blocks in pieces:
        steps = jnp.exp(jax.random.uniform(jax.random.fold_in(own, dim), (blocks,), jnp.float32, smallest / len(pieces), high / len(pieces)))
        factor_of = factor_of * jnp.repeat(steps, extent[dim] // blocks).reshape([-1 if axis == dim else 1 for axis in range(len(extent))])
    return factor_of


def normal_values(key, extent, scale, most, shards=(), held_as=jnp.bfloat16):
    gain = shard_levels(key, extent, shards, -0.22, 0.18) if shards else 1.0
    result = jax.random.normal(key, extent, jnp.float32) * scale * gain
    return jnp.minimum(jnp.maximum(result, -most), most).astype(held_as)


def setup_inputs(seed: int = 0, part: int = 0) -> dict:
    splits = jax.random.split(jax.random.key(seed), 13)
    part_keys = jax.random.split(jax.random.fold_in(splits[12], part), 13)
    return {
        "first_feat": draw_first_feat(jax.random.fold_in(jax.random.fold_in(splits[12], part), 71), part),
        "second_feat": draw_second_feat(jax.random.fold_in(jax.random.fold_in(splits[12], part), 71), part),
        "hidden_init": normal_values(part_keys[2], (BLOCKS, P_SIZE, C), 1.0, 4.0, ((0, 16),)),
        "cotangent": normal_values(part_keys[3], (BLOCKS, P_SIZE, C), 1.0, 6.0, ((0, 16),)),
        "search_list": draw_search_list(jax.random.fold_in(jax.random.fold_in(splits[12], part), 71), part),
        "offsets": plant(jax.random.randint(part_keys[5], (ITERS, BLOCKS), -1, 2), jax.random.fold_in(part_keys[5], 1), -1, 1).astype(jnp.int32),
        "lengths": draw_lengths(jax.random.fold_in(jax.random.fold_in(splits[12], part), 71), part),
        "hid_weight": normal_values(splits[7], (C, 2 * C), C ** -0.5, 0.375),
        "in_weight": normal_values(splits[8], (C, 3 * C), C ** -0.5, 0.375),
        "cand_weight": normal_values(splits[9], (C, C), C ** -0.5, 0.375),
        "disp_weight": normal_values(splits[10], (2, 3 * C), 0.3, 1.5, (), jnp.float32),
        "gate_bias": jnp.clip(jax.random.uniform(splits[11], (3 * C,), jnp.float32, -1.0, 1.0), -1.0, 1.0),
    }


def motion_update(hidden, motion_half, flow_rows, flow_cols, hid_weight, in_weight, cand_weight, disp_weight, gate_bias):
    channels = hidden.shape[1]
    from_hidden = jnp.dot(hidden.astype(jnp.bfloat16), hid_weight, preferred_element_type=jnp.float32)
    from_input = jnp.dot(motion_half, in_weight, preferred_element_type=jnp.float32)
    inputs = from_input + flow_rows[:, None] * disp_weight[0] + flow_cols[:, None] * disp_weight[1] + gate_bias
    update = jax.nn.sigmoid(from_hidden[:, :channels] + inputs[:, :channels])
    reset_gate = jax.nn.sigmoid(from_hidden[:, channels:] + inputs[:, channels:2 * channels])
    candidate = jnp.tanh(jnp.dot((reset_gate * hidden).astype(jnp.bfloat16), cand_weight, preferred_element_type=jnp.float32) + inputs[:, 2 * channels:])
    return (1.0 - update) * hidden + update * candidate

def displacement(weights, block_ids, global_ids, cell_count):
    cell_index = jnp.arange(cell_count, dtype=jnp.int32)
    key_row = ((block_ids // BW - global_ids[:, None] // BW) * PH)[:, :, None] + (cell_index // PW)[None, None, :]
    key_col = ((block_ids % BW - global_ids[:, None] % BW) * PW)[:, :, None] + (cell_index % PW)[None, None, :]
    key_y = key_row.astype(jnp.float32) / PH
    key_x = key_col.astype(jnp.float32) / PW
    flow_rows = lax.optimization_barrier(jnp.sum(weights * key_y[:, None], axis=(2, 3))) - (cell_index // PW).astype(jnp.float32)[None, :] / PH
    flow_cols = lax.optimization_barrier(jnp.sum(weights * key_x[:, None], axis=(2, 3))) - (cell_index % PW).astype(jnp.float32)[None, :] / PW
    return (flow_rows, flow_cols)

def attend(queries, key_blocks, live_slots, score_scale):
    scores = jnp.einsum('bpc,blkc->bplk', queries.astype(jnp.float32), key_blocks.astype(jnp.float32)) * score_scale
    scores = jnp.where(live_slots[:, None, :, None], scores, -jnp.inf)
    row_max = lax.optimization_barrier(jnp.max(scores, axis=(2, 3), keepdims=True))
    exponent = jnp.exp(scores - row_max)
    weights = exponent / lax.optimization_barrier(jnp.sum(exponent, axis=(2, 3), keepdims=True))
    half_weights = lax.optimization_barrier(weights.astype(jnp.bfloat16))
    motion = jnp.einsum('bplk,blkc->bpc', half_weights.astype(jnp.float32), key_blocks.astype(jnp.float32))
    return (weights, half_weights, motion)

def reference(first_feat, second_feat, hidden_init, cotangent, search_list, offsets, lengths, hid_weight, in_weight, cand_weight, disp_weight, gate_bias):
    row_count = BLOCKS // BW
    score_scale = 1.0 / math.sqrt(C)

    def shape_rows(array):
        return array.reshape((row_count, BW) + array.shape[1:])
    row_inputs = (shape_rows(first_feat), shape_rows(hidden_init), shape_rows(cotangent), shape_rows(search_list), shape_rows(jnp.transpose(offsets)), shape_rows(lengths), jnp.arange(row_count, dtype=jnp.int32))

    def row_step(grad_sum, inputs_row):
        feat_rows, start_rows, cot_rows, list_rows, shift_rows, length_rows, row_number = inputs_row
        global_ids = row_number * BW + jnp.arange(BW, dtype=jnp.int32)
        live_slots = jnp.arange(SLOTS, dtype=jnp.int32)[None, :] < length_rows[:, None]
        hidden = start_rows.reshape(BW * P_SIZE, C).astype(jnp.float32)
        for refine in range(ITERS):
            block_ids = (list_rows + shift_rows[:, refine][:, None]).astype(jnp.int32)
            key_blocks = second_feat[block_ids]
            queries = lax.optimization_barrier((feat_rows.astype(jnp.float32) + hidden.reshape(BW, P_SIZE, C)).astype(jnp.bfloat16))
            weights, half_weights, motion = attend(queries, key_blocks, live_slots, score_scale)
            flow_rows, flow_cols = displacement(weights, block_ids, global_ids, P_SIZE)
            hidden = motion_update(hidden, motion.astype(jnp.bfloat16).reshape(BW * P_SIZE, C), flow_rows.reshape(-1), flow_cols.reshape(-1), hid_weight, in_weight, cand_weight, disp_weight, gate_bias)
        weight_grad = jnp.einsum('bpc,blkc->bplk', cot_rows.astype(jnp.float32), key_blocks.astype(jnp.float32))
        row_delta = lax.optimization_barrier(jnp.sum(weights * weight_grad, axis=(2, 3), keepdims=True))
        dscore = lax.optimization_barrier((weights * (weight_grad - row_delta) * score_scale).astype(jnp.bfloat16))
        contrib = jnp.einsum('bplk,bpc->blkc', half_weights.astype(jnp.float32), cot_rows.astype(jnp.float32))
        contrib = contrib + jnp.einsum('bplk,bpc->blkc', dscore.astype(jnp.float32), queries.astype(jnp.float32))
        grad_sum = grad_sum.at[block_ids.reshape(-1)].add(contrib.reshape(BW * SLOTS, P_SIZE, C))
        flow_pair = jnp.stack([flow_rows, flow_cols], axis=1)
        return (grad_sum, (hidden.reshape(BW, P_SIZE, C), flow_pair))
    grad_sum, (hidden_rows, flow_pairs) = lax.scan(row_step, jnp.zeros((BLOCKS, P_SIZE, C), jnp.float32), row_inputs)
    return (hidden_rows.reshape(BLOCKS, P_SIZE, C), flow_pairs.reshape(BLOCKS, 2, P_SIZE), grad_sum)
```

```python
import functools
import math

import jax
import jax.numpy as jnp
from jax import lax
from jax.experimental import pallas as pl
from jax.experimental.pallas import tpu as pltpu
from jax.sharding import PartitionSpec as P

PH = 8
PW = 16
BW = 7
ITERS = 2
GROUP = 2
F32 = jnp.float32
BF16 = jnp.bfloat16


def dot_nt(a, b):
    return lax.dot_general(a, b, (((1,), (1,)), ((), ())), preferred_element_type=F32)


def dot_tn(a, b):
    return lax.dot_general(a, b, (((0,), (0,)), ((), ())), preferred_element_type=F32)


def sigmoid(x):
    return 0.5 * jnp.tanh(0.5 * x) + 0.5


def gates(h, motion, flow_r, flow_c, hid_w, in_w, cand_w, disp, bias):
    ch = h.shape[1]
    g = jnp.dot(h.astype(BF16), hid_w, preferred_element_type=F32)
    e = jnp.dot(motion, in_w, preferred_element_type=F32)
    e = e + (flow_r * disp[0:1] + (flow_c * disp[1:2] + bias))
    z = sigmoid(g[:, :ch] + e[:, :ch])
    r = sigmoid(g[:, ch:] + e[:, ch : 2 * ch])
    c = jnp.tanh(
        jnp.dot((r * h).astype(BF16), cand_w, preferred_element_type=F32) + e[:, 2 * ch :]
    )
    return h + z * (c - h)


def slot_places(search, offs, refine, b, slots, base):
    return [search[b, l] + offs[refine, b] - base for l in range(slots)]


def attention(q, keys, places, length, row_at, col_at):
    slots = len(places)
    cells = q.shape[0]
    scale = 1.0 / math.sqrt(q.shape[1])
    s = dot_nt(q, keys) * scale
    parts = [s[:, l * cells : (l + 1) * cells] for l in range(slots)]
    for l in range(1, slots):
        parts[l] = parts[l] + jnp.where(l < length, 0.0, -1e30).astype(F32)
    top = functools.reduce(jnp.maximum, parts)
    m = jnp.max(top, axis=1, keepdims=True)
    exps = [jnp.exp(p - m) for p in parts]
    total = jnp.sum(functools.reduce(jnp.add, exps), axis=1, keepdims=True)
    inv = 1.0 / total
    w = [x * inv for x in exps]
    half = [x.astype(BF16) for x in w]
    motion = jnp.dot(jnp.concatenate(half, axis=1), keys, preferred_element_type=F32)
    k = lax.broadcasted_iota(jnp.int32, (1, cells), 1)
    ky = (k // PW).astype(F32) / PH
    kx = (k % PW).astype(F32) / PW
    fr = fc = None
    for l in range(slots):
        row = (places[l] * 9363) >> 16
        col = places[l] - row * BW
        y = w[l] * (ky + (row - row_at).astype(F32))
        x = w[l] * (kx + (col - col_at).astype(F32))
        fr, fc = (y, x) if l == 0 else (fr + y, fc + x)
    p = lax.broadcasted_iota(jnp.int32, (cells, 1), 0)
    fr = jnp.sum(fr, axis=1, keepdims=True) - (p // PW).astype(F32) / PH
    fc = jnp.sum(fc, axis=1, keepdims=True) - (p % PW).astype(F32) / PW
    return w, half, motion.astype(BF16), fr, fc


def main_kernel(
    search, offs, lens, first_h, before_h, second_h, after_h, hidden_h, cot_h,
    hid_w, in_w, cand_w, disp, bias,
    h_out, mot_out, fcol_out, flow_out, own_out, low_out, up_out,
    win, first, hid0, cot, acc, sems,
):
    blocks, cells, ch = first_h.shape
    slots = search.shape[1]
    copies = [
        pltpu.make_async_copy(second_h, win.at[pl.ds(BW, blocks)], sems.at[0]),
        pltpu.make_async_copy(before_h, win.at[pl.ds(0, BW)], sems.at[1]),
        pltpu.make_async_copy(after_h, win.at[pl.ds(BW + blocks, BW)], sems.at[2]),
        pltpu.make_async_copy(first_h, first, sems.at[3]),
        pltpu.make_async_copy(hidden_h, hid0, sems.at[4]),
        pltpu.make_async_copy(cot_h, cot, sems.at[5]),
    ]
    for c in copies:
        c.start()
    base = lax.axis_index("tile") * blocks - BW
    acc[...] = jnp.zeros_like(acc)
    for c in copies:
        c.wait()

    def body(step, carry):
        bs = [step * GROUP + j for j in range(GROUP)]
        at = [slot_row_col(b) for b in bs]
        h = [hid0[b].astype(F32) for b in bs]
        for refine in range(ITERS):
            outs = []
            for j, b in enumerate(bs):
                places = slot_places(search, offs, refine, b, slots, base)
                keys = jnp.concatenate([win[i] for i in places], axis=0)
                q = (first[b].astype(F32) + h[j]).astype(BF16)
                w, half, motion, fr, fc = attention(q, keys, places, lens[b], *at[j])
                outs.append((motion, fr, fc))
                if refine == ITERS - 1:
                    ct = cot[b]
                    dw = dot_nt(ct, keys)
                    dws = [dw[:, l * cells : (l + 1) * cells] for l in range(slots)]
                    prod = functools.reduce(jnp.add, [w[l] * dws[l] for l in range(slots)])
                    delta = jnp.sum(prod, axis=1, keepdims=True)
                    ds = [
                        (w[l] * (dws[l] - delta) * (1.0 / math.sqrt(ch))).astype(BF16)
                        for l in range(slots)
                    ]
                    stacked = jnp.concatenate(
                        [jnp.concatenate(half, axis=1), jnp.concatenate(ds, axis=1)], axis=0
                    )
                    contrib = dot_tn(stacked, jnp.concatenate([ct, q], axis=0))
                    for l in range(slots):
                        acc[places[l]] += contrib[l * cells : (l + 1) * cells]
            motion, fr, fc = (jnp.concatenate(t, axis=0) for t in zip(*outs))
            if refine < ITERS - 1:
                hcat = jnp.concatenate(h, axis=0)
                hcat = gates(
                    hcat, motion, fr, fc, hid_w[...], in_w[...], cand_w[...], disp[...], bias[...]
                )
                h = [hcat[j * cells : (j + 1) * cells] for j in range(GROUP)]
            else:
                lane = lax.broadcasted_iota(jnp.int32, (cells, cells), 1)
                for j, b in enumerate(bs):
                    mot_out[b] = outs[j][0]
                    h_out[b] = h[j]
                    both = jnp.where(lane == 0, outs[j][1], outs[j][2])
                    fcol_out[b] = both
                    flow_out[b] = both.T[0:2]
        return carry

    lax.fori_loop(0, blocks // GROUP, body, 0)
    own_out[...] = acc[BW : BW + blocks]
    low_out[...] = acc[0:BW].astype(BF16)
    up_out[...] = acc[BW + blocks :].astype(BF16)


def slot_row_col(b):
    row = (b * 9363) >> 16
    return row + 1, b - row * BW


def last_gates_kernel(h, mot, fcol, hid_w, in_w, cand_w, disp, bias, out):
    g, cells, ch = h.shape
    f = fcol[...].reshape(g * cells, cells)
    res = gates(
        h[...].reshape(g * cells, ch),
        mot[...].reshape(g * cells, ch),
        f[:, 0:1],
        f[:, 1:2],
        hid_w[...], in_w[...], cand_w[...], disp[...], bias[...],
    )
    out[...] = res.reshape(g, cells, ch)


def local(
    first_feat, second_feat, hidden_init, cotangent, search_list, offsets, lengths,
    hid_weight, in_weight, cand_weight, disp_weight, gate_bias,
):
    blocks, cells, ch = first_feat.shape
    n = lax.axis_size("tile")
    up = [(i, i + 1) for i in range(n - 1)]
    down = [(i + 1, i) for i in range(n - 1)]
    before = lax.ppermute(second_feat[blocks - BW :], "tile", up)
    after = lax.ppermute(second_feat[:BW], "tile", down)
    bias = gate_bias.reshape(1, -1)
    smem = pl.BlockSpec(memory_space=pltpu.SMEM)
    hbm = pl.BlockSpec(memory_space=pl.ANY)
    vmem = pl.BlockSpec(memory_space=pltpu.VMEM)
    sds = jax.ShapeDtypeStruct
    macs = blocks * cells * (4 * cells * ch * 7 + ch * ch * 6)
    h1, mot, fcol, flow, own, low, high = pl.pallas_call(
        main_kernel,
        out_shape=[
            sds((blocks, cells, ch), F32),
            sds((blocks, cells, ch), BF16),
            sds((blocks, cells, cells), F32),
            sds((blocks, 2, cells), F32),
            sds((blocks, cells, ch), F32),
            sds((BW, cells, ch), BF16),
            sds((BW, cells, ch), BF16),
        ],
        in_specs=[smem] * 3 + [hbm] * 6 + [vmem] * 5,
        out_specs=[vmem] * 7,
        scratch_shapes=[
            pltpu.VMEM((blocks + 2 * BW, cells, ch), BF16),
            pltpu.VMEM((blocks, cells, ch), BF16),
            pltpu.VMEM((blocks, cells, ch), BF16),
            pltpu.VMEM((blocks, cells, ch), BF16),
            pltpu.VMEM((blocks + 2 * BW, cells, ch), F32),
            pltpu.SemaphoreType.DMA((6,)),
        ],
        compiler_params=pltpu.CompilerParams(vmem_limit_bytes=48 * 2**20),
        cost_estimate=pl.CostEstimate(flops=2 * macs, bytes_accessed=10 * 2**20, transcendentals=0),
    )(
        search_list, offsets, lengths, first_feat, before, second_feat, after,
        hidden_init, cotangent, hid_weight, in_weight, cand_weight, disp_weight, bias,
    )
    from_next = lax.ppermute(low, "tile", down)
    from_prev = lax.ppermute(high, "tile", up)
    step = lambda i: (i, 0, 0)
    whole = lambda i: (0, 0)
    hidden = pl.pallas_call(
        last_gates_kernel,
        out_shape=sds((blocks, cells, ch), F32),
        grid=(blocks // GROUP,),
        in_specs=[
            pl.BlockSpec((GROUP, cells, ch), step),
            pl.BlockSpec((GROUP, cells, ch), step),
            pl.BlockSpec((GROUP, cells, cells), step),
            pl.BlockSpec(hid_weight.shape, whole),
            pl.BlockSpec(in_weight.shape, whole),
            pl.BlockSpec(cand_weight.shape, whole),
            pl.BlockSpec(disp_weight.shape, whole),
            pl.BlockSpec(bias.shape, whole),
        ],
        out_specs=pl.BlockSpec((GROUP, cells, ch), step),
        compiler_params=pltpu.CompilerParams(vmem_limit_bytes=24 * 2**20),
        cost_estimate=pl.CostEstimate(
            flops=2 * blocks * cells * ch * ch * 6, bytes_accessed=5 * 2**20, transcendentals=0
        ),
    )(h1, mot, fcol, hid_weight, in_weight, cand_weight, disp_weight, bias)
    own = jnp.concatenate(
        [own[:BW] + from_prev.astype(F32), own[BW:-BW], own[-BW:] + from_next.astype(F32)], axis=0
    ) if blocks > 2 * BW else jnp.concatenate(
        [own[:BW] + from_prev.astype(F32), own[BW:] + from_next.astype(F32)], axis=0
    )
    return hidden, flow, own


def solution(mesh):
    lead = ("grp", "tile")
    return jax.shard_map(
        local,
        mesh=mesh,
        in_specs=(
            P(lead, None, None), P(lead, None, None), P(lead, None, None), P(lead, None, None),
            P(lead, None), P(None, lead), P(lead), P(), P(), P(), P(), P(),
        ),
        out_specs=(P(lead, None, None), P(lead, None, None), P(lead, None, None)),
        check_vma=False,
    )
```

```python
import functools
import math

import jax
import jax.numpy as jnp
from jax import lax
from jax.experimental import pallas as pl
from jax.experimental.pallas import tpu as pltpu
from jax.sharding import PartitionSpec as P

PH = 8
PW = 16
BW = 7
ITERS = 2
GROUP = 2
F32 = jnp.float32
BF16 = jnp.bfloat16
MESH = pl.DeviceIdType.MESH


def dot_nt(a, b):
    return lax.dot_general(a, b, (((1,), (1,)), ((), ())), preferred_element_type=F32)


def dot_tn(a, b):
    return lax.dot_general(a, b, (((0,), (0,)), ((), ())), preferred_element_type=F32)


def sigmoid(x):
    return 0.5 * jnp.tanh(0.5 * x) + 0.5


def gates(h, g, motion, flow_r, flow_c, in_w, cand_w, disp, bias):
    ch = h.shape[1]
    e = jnp.dot(motion, in_w, preferred_element_type=F32)
    e = e + (flow_r * disp[0:1] + (flow_c * disp[1:2] + bias))
    z = sigmoid(g[:, :ch] + e[:, :ch])
    r = sigmoid(g[:, ch:] + e[:, ch : 2 * ch])
    c = jnp.tanh(
        jnp.dot((r * h).astype(BF16), cand_w, preferred_element_type=F32) + e[:, 2 * ch :]
    )
    return h + z * (c - h)


def slot_places(search, offs, refine, b, slots, base, span):
    at = [search[b, l] + offs[refine, b] - base for l in range(slots)]
    return [jnp.minimum(jnp.maximum(i, 0), span - 1) for i in at]


def attention(q, keys, places, length, row_at, col_at):
    slots = len(places)
    cells = q.shape[0]
    scale = 1.0 / math.sqrt(q.shape[1])
    s = dot_nt(q, keys) * scale
    parts = [s[:, l * cells : (l + 1) * cells] for l in range(slots)]
    for l in range(1, slots):
        parts[l] = parts[l] + jnp.where(l < length, 0.0, -1e30).astype(F32)
    top = functools.reduce(jnp.maximum, parts)
    m = jnp.max(top, axis=1, keepdims=True)
    exps = [jnp.exp(p - m) for p in parts]
    total = jnp.sum(functools.reduce(jnp.add, exps), axis=1, keepdims=True)
    inv = 1.0 / total
    w = [x * inv for x in exps]
    half = [x.astype(BF16) for x in w]
    motion = jnp.dot(jnp.concatenate(half, axis=1), keys, preferred_element_type=F32)
    k = lax.broadcasted_iota(jnp.int32, (1, cells), 1)
    ky = (k // PW).astype(F32) / PH
    kx = (k % PW).astype(F32) / PW
    fr = fc = None
    for l in range(slots):
        row = (places[l] * 9363) >> 16
        col = places[l] - row * BW
        y = w[l] * (ky + (row - row_at).astype(F32))
        x = w[l] * (kx + (col - col_at).astype(F32))
        fr, fc = (y, x) if l == 0 else (fr + y, fc + x)
    p = lax.broadcasted_iota(jnp.int32, (cells, 1), 0)
    fr = jnp.sum(fr, axis=1, keepdims=True) - (p // PW).astype(F32) / PH
    fc = jnp.sum(fc, axis=1, keepdims=True) - (p % PW).astype(F32) / PW
    return w, half, motion.astype(BF16), fr, fc


def slot_row_col(b):
    row = (b * 9363) >> 16
    return row + 1, b - row * BW


def main_kernel(
    count, search, offs, lens, prev, last, first_h, second_h, hidden_h, cot_h, hid_h, in_h, cand_h,
    disp, bias,
    hid_out, flow_out, own_out, low_in, high_in,
    win, first, hid0, cot, hid_w, in_w, cand_w, con, hbuf, mot, fcol, gbuf, own, stage,
    sems, out_sems, send_sems, recv_sems,
):
    blocks, cells, ch = first_h.shape
    slots = search.shape[1]
    spare = blocks * slots
    me = lax.axis_index("tile")
    has_prev = me > 0
    has_next = me < count - 1

    barrier = pltpu.get_barrier_semaphore()

    @pl.when(has_prev)
    def _():
        pl.semaphore_signal(barrier, inc=1, device_id={"tile": me - 1}, device_id_type=MESH)

    @pl.when(has_next)
    def _():
        pl.semaphore_signal(barrier, inc=1, device_id={"tile": me + 1}, device_id_type=MESH)

    def local_copy(src, dst, k):
        c = pltpu.make_async_copy(src, dst, sems.at[k])
        c.start()
        return c

    hid_copies = [local_copy(hidden_h, hid0, 0), local_copy(hid_h, hid_w, 1)]

    def remote(src, dst, k, target):
        return pltpu.make_async_remote_copy(
            src_ref=src, dst_ref=dst, send_sem=send_sems.at[k], recv_sem=recv_sems.at[k],
            device_id={"tile": target}, device_id_type=MESH,
        )

    halo_up = remote(second_h.at[pl.ds(blocks - BW, BW)], win.at[pl.ds(0, BW)], 0, me + 1)
    halo_down = remote(second_h.at[pl.ds(0, BW)], win.at[pl.ds(BW + blocks, BW)], 1, me - 1)

    pl.semaphore_wait(barrier, has_prev.astype(jnp.int32) + has_next.astype(jnp.int32))

    @pl.when(has_next)
    def _():
        halo_up.start()

    @pl.when(has_prev)
    def _():
        halo_down.start()

    copies = [
        local_copy(second_h, win.at[pl.ds(BW, blocks)], 2),
        local_copy(first_h, first, 3),
        local_copy(cot_h, cot, 4),
        local_copy(in_h, in_w, 5),
        local_copy(cand_h, cand_w, 6),
    ]
    base = me * blocks - BW
    con[spare] = jnp.zeros((cells, ch), F32)
    for c in hid_copies:
        c.wait()

    def early(b, carry):
        gbuf[b] = jnp.dot(hid0[b], hid_w[...], preferred_element_type=F32)
        return carry

    lax.fori_loop(0, blocks, early, 0)
    for c in copies:
        c.wait()

    @pl.when(has_prev)
    def _():
        halo_up.wait_recv()

    @pl.when(has_next)
    def _():
        halo_down.wait_recv()

    def body(step, carry):
        bs = [step * GROUP + j for j in range(GROUP)]
        at = [slot_row_col(b) for b in bs]
        h = [hid0[b].astype(F32) for b in bs]
        for refine in range(ITERS):
            outs = []
            for j, b in enumerate(bs):
                places = slot_places(search, offs, refine, b, slots, base, win.shape[0])
                keys = jnp.concatenate([win[i] for i in places], axis=0)
                q = (first[b].astype(F32) + h[j]).astype(BF16)
                w, half, motion, fr, fc = attention(q, keys, places, lens[b], *at[j])
                outs.append((motion, fr, fc))
                if refine == ITERS - 1:
                    ct = cot[b]
                    dw = dot_nt(ct, keys)
                    dws = [dw[:, l * cells : (l + 1) * cells] for l in range(slots)]
                    prod = functools.reduce(jnp.add, [w[l] * dws[l] for l in range(slots)])
                    delta = jnp.sum(prod, axis=1, keepdims=True)
                    ds = [
                        (w[l] * (dws[l] - delta) * (1.0 / math.sqrt(ch))).astype(BF16)
                        for l in range(slots)
                    ]
                    stacked = jnp.concatenate(
                        [jnp.concatenate(half, axis=1), jnp.concatenate(ds, axis=1)], axis=0
                    )
                    contrib = dot_tn(stacked, jnp.concatenate([ct, q], axis=0))
                    for l in range(slots):
                        con[b * slots + l] = (
                            contrib[l * cells : (l + 1) * cells] + con[prev[b * slots + l]]
                        )
            if refine < ITERS - 1:
                motion, fr, fc = (jnp.concatenate(t, axis=0) for t in zip(*outs))
                hcat = jnp.concatenate(h, axis=0)
                g = jnp.concatenate([gbuf[b] for b in bs], axis=0)
                hcat = gates(
                    hcat, g, motion, fr, fc, in_w[...], cand_w[...], disp[...], bias[...]
                )
                h = [hcat[j * cells : (j + 1) * cells] for j in range(GROUP)]
            else:
                lane = lax.broadcasted_iota(jnp.int32, (cells, cells), 1)
                for j, b in enumerate(bs):
                    mot[b] = outs[j][0]
                    hbuf[b] = h[j]
                    both = jnp.where(lane == 0, outs[j][1], outs[j][2])
                    fcol[b] = both
                    flow_out[b] = both.T[0:2]
        return carry

    lax.fori_loop(0, blocks // GROUP, body, 0)

    for i in range(BW):
        stage[1, i] = con[last[BW + blocks + i]].astype(BF16)
    grad_up = remote(stage.at[1], low_in, 2, me + 1)

    @pl.when(has_next)
    def _():
        grad_up.start()

    for i in range(BW):
        stage[0, i] = con[last[i]].astype(BF16)
    grad_down = remote(stage.at[0], high_in, 3, me - 1)

    @pl.when(has_prev)
    def _():
        grad_down.start()

    def gather(i, carry):
        own[i] = con[last[BW + i]]
        return carry

    lax.fori_loop(0, blocks, gather, 0)
    own_copy = local_copy(own, own_out, 0)

    def late(step, carry):
        rows = pl.ds(step * GROUP, GROUP)
        h = hbuf[rows].reshape(GROUP * cells, ch)
        f = fcol[rows].reshape(GROUP * cells, cells)
        g = jnp.dot(h.astype(BF16), hid_w[...], preferred_element_type=F32)
        res = gates(
            h, g, mot[rows].reshape(GROUP * cells, ch), f[:, 0:1], f[:, 1:2],
            in_w[...], cand_w[...], disp[...], bias[...],
        )
        hbuf[rows] = res.reshape(GROUP, cells, ch)
        pltpu.make_async_copy(hbuf.at[rows], hid_out.at[rows], out_sems.at[step]).start()
        return carry

    lax.fori_loop(0, blocks // GROUP, late, 0)

    def drain(step, carry):
        rows = pl.ds(step * GROUP, GROUP)
        pltpu.make_async_copy(hbuf.at[rows], hid_out.at[rows], out_sems.at[step]).wait()
        return carry

    lax.fori_loop(0, blocks // GROUP, drain, 0)
    own_copy.wait()

    @pl.when(has_next)
    def _():
        halo_up.wait_send()
        grad_up.wait_send()
        grad_down.wait_recv()

    @pl.when(has_prev)
    def _():
        halo_down.wait_send()
        grad_down.wait_send()
        grad_up.wait_recv()


def local(
    first_feat, second_feat, hidden_init, cotangent, search_list, offsets, lengths,
    hid_weight, in_weight, cand_weight, disp_weight, gate_bias,
):
    blocks, cells, ch = first_feat.shape
    slots = search_list.shape[1]
    n = lax.axis_size("tile")
    me = lax.axis_index("tile")
    span = blocks + 2 * BW
    spare = blocks * slots
    place = (search_list + offsets[ITERS - 1][:, None]).reshape(-1) - me * blocks + BW
    t = jnp.arange(spare, dtype=jnp.int32)
    wanted = jnp.concatenate([place, jnp.arange(span, dtype=jnp.int32)])
    limit = jnp.concatenate([t, jnp.full((span,), spare, jnp.int32)])
    hit = (place[None, :] == wanted[:, None]) & (t[None, :] < limit[:, None])
    found = jnp.max(jnp.where(hit, t[None, :], -1), axis=1)
    found = jnp.where(found < 0, spare, found)
    prev, last = found[:spare], found[spare:]
    bias = gate_bias.reshape(1, -1)
    smem = pl.BlockSpec(memory_space=pltpu.SMEM)
    hbm = pl.BlockSpec(memory_space=pl.ANY)
    vmem = pl.BlockSpec(memory_space=pltpu.VMEM)
    sds = jax.ShapeDtypeStruct
    macs = blocks * cells * (4 * cells * ch * 7 + ch * ch * 12)
    hidden, flow, own, low, high = pl.pallas_call(
        functools.partial(main_kernel, n),
        out_shape=[
            sds((blocks, cells, ch), F32),
            sds((blocks, 2, cells), F32),
            sds((blocks, cells, ch), F32),
            sds((BW, cells, ch), BF16),
            sds((BW, cells, ch), BF16),
        ],
        in_specs=[smem] * 5 + [hbm] * 7 + [vmem] * 2,
        out_specs=[hbm, vmem, hbm, hbm, hbm],
        scratch_shapes=[
            pltpu.VMEM((span, cells, ch), BF16),
            pltpu.VMEM((blocks, cells, ch), BF16),
            pltpu.VMEM((blocks, cells, ch), BF16),
            pltpu.VMEM((blocks, cells, ch), BF16),
            pltpu.VMEM(hid_weight.shape, BF16),
            pltpu.VMEM(in_weight.shape, BF16),
            pltpu.VMEM(cand_weight.shape, BF16),
            pltpu.VMEM((spare + 1, cells, ch), F32),
            pltpu.VMEM((blocks, cells, ch), F32),
            pltpu.VMEM((blocks, cells, ch), BF16),
            pltpu.VMEM((blocks, cells, cells), F32),
            pltpu.VMEM((blocks, cells, 2 * ch), F32),
            pltpu.VMEM((blocks, cells, ch), F32),
            pltpu.VMEM((2, BW, cells, ch), BF16),
            pltpu.SemaphoreType.DMA((7,)),
            pltpu.SemaphoreType.DMA((blocks // GROUP,)),
            pltpu.SemaphoreType.DMA((4,)),
            pltpu.SemaphoreType.DMA((4,)),
        ],
        compiler_params=pltpu.CompilerParams(
            vmem_limit_bytes=52 * 2**20, collective_id=0, has_side_effects=True
        ),
        cost_estimate=pl.CostEstimate(flops=2 * macs, bytes_accessed=10 * 2**20, transcendentals=0),
    )(
        search_list, offsets, lengths, prev, last, first_feat, second_feat,
        hidden_init, cotangent, hid_weight, in_weight, cand_weight, disp_weight, bias,
    )
    from_prev = jnp.where(me > 0, low.astype(F32), 0.0)
    from_next = jnp.where(me < n - 1, high.astype(F32), 0.0)
    own = jnp.concatenate(
        [own[:BW] + from_prev, own[BW : blocks - BW], own[blocks - BW :] + from_next], axis=0
    )
    return hidden, flow, own


def solution(mesh):
    lead = ("grp", "tile")
    return jax.shard_map(
        local,
        mesh=mesh,
        in_specs=(
            P(lead, None, None), P(lead, None, None), P(lead, None, None), P(lead, None, None),
            P(lead, None), P(None, lead), P(lead), P(), P(), P(), P(), P(),
        ),
        out_specs=(P(lead, None, None), P(lead, None, None), P(lead, None, None)),
        check_vma=False,
    )
```

```python
import functools
import math

import jax
import jax.numpy as jnp
from jax import lax
from jax.experimental import pallas as pl
from jax.experimental.pallas import tpu as pltpu
from jax.sharding import PartitionSpec as P

PH = 8
PW = 16
BW = 7
ITERS = 2
GROUP = 2
WIDTH = 2
F32 = jnp.float32
BF16 = jnp.bfloat16
MESH = pl.DeviceIdType.MESH


def dot_nt(a, b):
    return lax.dot_general(a, b, (((1,), (1,)), ((), ())), preferred_element_type=F32)


def dot_tn(a, b):
    return lax.dot_general(a, b, (((0,), (0,)), ((), ())), preferred_element_type=F32)


def sigmoid(x):
    return 0.5 * jnp.tanh(0.5 * x) + 0.5


def gates(h, g, motion, flow_r, flow_c, in_w, cand_w, disp, bias):
    ch = h.shape[1]
    e = jnp.dot(motion, in_w, preferred_element_type=F32)
    e = e + (flow_r * disp[0:1] + (flow_c * disp[1:2] + bias))
    z = sigmoid(g[:, :ch] + e[:, :ch])
    r = sigmoid(g[:, ch:] + e[:, ch : 2 * ch])
    c = jnp.tanh(
        jnp.dot((r * h).astype(BF16), cand_w, preferred_element_type=F32) + e[:, 2 * ch :]
    )
    return h + z * (c - h)


def slot_places(search, offs, refine, b, slots, base, span):
    at = [search[l, b] + offs[refine, b] - base for l in range(slots)]
    return [jnp.minimum(jnp.maximum(i, 0), span - 1) for i in at]


def attention(q, keys, places, length, row_at, col_at):
    slots = len(places)
    cells = q.shape[0]
    scale = 1.0 / math.sqrt(q.shape[1])
    s = dot_nt(q, keys) * scale
    parts = [s[:, l * cells : (l + 1) * cells] for l in range(slots)]
    for l in range(1, slots):
        parts[l] = parts[l] + jnp.where(l < length, 0.0, -1e30).astype(F32)
    top = functools.reduce(jnp.maximum, parts)
    m = jnp.max(top, axis=1, keepdims=True)
    exps = [jnp.exp(p - m) for p in parts]
    total = jnp.sum(functools.reduce(jnp.add, exps), axis=1, keepdims=True)
    inv = 1.0 / total
    w = [x * inv for x in exps]
    half = [x.astype(BF16) for x in w]
    motion = jnp.dot(jnp.concatenate(half, axis=1), keys, preferred_element_type=F32)
    k = lax.broadcasted_iota(jnp.int32, (1, cells), 1)
    ky = (k // PW).astype(F32) / PH
    kx = (k % PW).astype(F32) / PW
    fr = fc = None
    for l in range(slots):
        row = (places[l] * 9363) >> 16
        col = places[l] - row * BW
        y = w[l] * (ky + (row - row_at).astype(F32))
        x = w[l] * (kx + (col - col_at).astype(F32))
        fr, fc = (y, x) if l == 0 else (fr + y, fc + x)
    p = lax.broadcasted_iota(jnp.int32, (cells, 1), 0)
    fr = jnp.sum(fr, axis=1, keepdims=True) - (p // PW).astype(F32) / PH
    fc = jnp.sum(fc, axis=1, keepdims=True) - (p % PW).astype(F32) / PW
    return w, half, motion.astype(BF16), fr, fc


def slot_row_col(b):
    row = (b * 9363) >> 16
    return row + 1, b - row * BW


def main_kernel(
    count, search, offs, lens, prev, last, first_h, second_h, hidden_h, cot_h, hid_h, in_h, cand_h,
    disp, bias,
    hid_out, flow_out, own_out, low_in, high_in,
    win, front, first, hid0, cot, hid_w, in_w, cand_w, con, hbuf, mot, fcol, gbuf, own, stage,
    sems, out_sems, send_sems, recv_sems,
):
    blocks, cells, ch = first_h.shape
    slots = search.shape[0]
    spare = blocks * slots
    me = lax.axis_index("tile")
    has_prev = me > 0
    has_next = me < count - 1

    barrier = pltpu.get_barrier_semaphore()

    @pl.when(has_prev)
    def _():
        pl.semaphore_signal(barrier, inc=1, device_id={"tile": me - 1}, device_id_type=MESH)

    @pl.when(has_next)
    def _():
        pl.semaphore_signal(barrier, inc=1, device_id={"tile": me + 1}, device_id_type=MESH)

    def local_copy(src, dst, k):
        c = pltpu.make_async_copy(src, dst, sems.at[k])
        c.start()
        return c

    hid_copies = [local_copy(hidden_h, hid0, 0), local_copy(hid_h, hid_w, 1)]

    def remote(src, dst, k, target):
        return pltpu.make_async_remote_copy(
            src_ref=src, dst_ref=dst, send_sem=send_sems.at[k], recv_sem=recv_sems.at[k],
            device_id={"tile": target}, device_id_type=MESH,
        )

    halo_up = remote(second_h.at[pl.ds(blocks - BW, BW)], front, 0, me + 1)
    halo_down = remote(second_h.at[pl.ds(0, BW)], win.at[pl.ds(BW + blocks, BW)], 1, me - 1)

    pl.semaphore_wait(barrier, has_prev.astype(jnp.int32) + has_next.astype(jnp.int32))

    @pl.when(has_prev)
    def _():
        halo_down.start()

    copies = [
        local_copy(second_h, win.at[pl.ds(BW, blocks)], 2),
        local_copy(first_h, first, 3),
        local_copy(cot_h, cot, 4),
        local_copy(in_h, in_w, 5),
        local_copy(cand_h, cand_w, 6),
    ]
    base = me * blocks - BW
    con[spare] = jnp.zeros((cells, ch), F32)
    for c in hid_copies:
        c.wait()

    def early(b, carry):
        gbuf[b] = jnp.dot(hid0[b], hid_w[...], preferred_element_type=F32)
        return carry

    lax.fori_loop(0, blocks, early, 0)
    for c in copies:
        c.wait()

    @pl.when(has_next)
    def _():
        halo_down.wait_recv()
        halo_up.start()

    def body(start, width):
        bs = [start + j for j in range(width)]
        at = [slot_row_col(b) for b in bs]
        h = [hid0[b].astype(F32) for b in bs]
        for refine in range(ITERS):
            outs = []
            for j, b in enumerate(bs):
                places = slot_places(search, offs, refine, b, slots, base, win.shape[0])
                keys = jnp.concatenate([win[i] for i in places], axis=0)
                q = (first[b].astype(F32) + h[j]).astype(BF16)
                w, half, motion, fr, fc = attention(q, keys, places, lens[b], *at[j])
                outs.append((motion, fr, fc))
                if refine == ITERS - 1:
                    ct = cot[b]
                    dw = dot_nt(ct, keys)
                    dws = [dw[:, l * cells : (l + 1) * cells] for l in range(slots)]
                    prod = functools.reduce(jnp.add, [w[l] * dws[l] for l in range(slots)])
                    delta = jnp.sum(prod, axis=1, keepdims=True)
                    ds = [
                        (w[l] * (dws[l] - delta) * (1.0 / math.sqrt(ch))).astype(BF16)
                        for l in range(slots)
                    ]
                    stacked = jnp.concatenate(
                        [jnp.concatenate(half, axis=1), jnp.concatenate(ds, axis=1)], axis=0
                    )
                    contrib = dot_tn(stacked, jnp.concatenate([ct, q], axis=0))
                    for l in range(slots):
                        con[turn_of(b) * slots + l] = (
                            contrib[l * cells : (l + 1) * cells] + con[prev[l, b]]
                        )
            if refine < ITERS - 1:
                motion, fr, fc = (jnp.concatenate(t, axis=0) for t in zip(*outs))
                hcat = jnp.concatenate(h, axis=0)
                g = jnp.concatenate([gbuf[b] for b in bs], axis=0)
                hcat = gates(
                    hcat, g, motion, fr, fc, in_w[...], cand_w[...], disp[...], bias[...].reshape(1, -1)
                )
                h = [hcat[j * cells : (j + 1) * cells] for j in range(width)]
            else:
                lane = lax.broadcasted_iota(jnp.int32, (cells, cells), 1)
                for j, b in enumerate(bs):
                    mot[b] = outs[j][0]
                    hbuf[b] = h[j]
                    both = jnp.where(lane == 0, outs[j][1], outs[j][2])
                    fcol[b] = both
                    flow_out[b] = both.T[0:2]

    def turn_of(b):
        return b + blocks - BW if isinstance(b, int) and b < BW else b - BW

    def run_row(start):
        for at in range(start, start + BW, WIDTH):
            body(at, min(WIDTH, start + BW - at))

    grad_up = remote(stage.at[1], low_in, 2, me + 1)
    grad_down = remote(stage.at[0], high_in, 3, me - 1)

    run_row(blocks - BW)
    for i in range(BW):
        stage[1, i] = con[last[BW + blocks + i]].astype(BF16)

    @pl.when(has_prev)
    def _():
        halo_up.wait_recv()
        win[0:BW] = front[...]

    @pl.when(has_next)
    def _():
        grad_up.start()

    run_row(0)
    for i in range(BW):
        stage[0, i] = con[last[i]].astype(BF16)

    @pl.when(has_prev)
    def _():
        grad_down.start()

    def gather(i, carry):
        own[i] = con[last[BW + i]]
        return carry

    lax.fori_loop(0, blocks, gather, 0)
    own_copy = local_copy(own, own_out, 0)

    def late(step, carry):
        rows = pl.ds(step * GROUP, GROUP)
        h = hbuf[rows].reshape(GROUP * cells, ch)
        f = fcol[rows].reshape(GROUP * cells, cells)
        g = jnp.dot(h.astype(BF16), hid_w[...], preferred_element_type=F32)
        res = gates(
            h, g, mot[rows].reshape(GROUP * cells, ch), f[:, 0:1], f[:, 1:2],
            in_w[...], cand_w[...], disp[...], bias[...].reshape(1, -1),
        )
        hbuf[rows] = res.reshape(GROUP, cells, ch)
        pltpu.make_async_copy(hbuf.at[rows], hid_out.at[rows], out_sems.at[step]).start()
        return carry

    lax.fori_loop(0, blocks // GROUP, late, 0)

    def drain(step, carry):
        rows = pl.ds(step * GROUP, GROUP)
        pltpu.make_async_copy(hbuf.at[rows], hid_out.at[rows], out_sems.at[step]).wait()
        return carry

    lax.fori_loop(0, blocks // GROUP, drain, 0)
    own_copy.wait()

    @pl.when(has_next)
    def _():
        halo_up.wait_send()
        grad_up.wait_send()
        grad_down.wait_recv()

    @pl.when(has_prev)
    def _():
        halo_down.wait_send()
        grad_down.wait_send()
        grad_up.wait_recv()


def local(
    first_feat, second_feat, hidden_init, cotangent, search_list, offsets, lengths,
    hid_weight, in_weight, cand_weight, disp_weight, gate_bias,
):
    blocks, cells, ch = first_feat.shape
    slots = search_list.shape[1]
    n = lax.axis_size("tile")
    me = lax.axis_index("tile")
    span = blocks + 2 * BW
    spare = blocks * slots
    listed = search_list.T
    place = listed + offsets[ITERS - 1][None, :] - me * blocks + BW
    slot = lax.broadcasted_iota(jnp.int32, (slots, blocks), 0)
    order = lax.broadcasted_iota(jnp.int32, (slots, blocks), 1)
    turn = jnp.where(order < BW, order + blocks - BW, order - BW) * slots + slot
    earlier = turn[None, None] < turn[:, :, None, None]
    same = (place[None, None] == place[:, :, None, None]) & earlier
    prev = jnp.max(jnp.where(same, turn[None, None], -1), axis=(2, 3))
    prev = jnp.where(prev < 0, spare, prev)
    hit = place[None] == lax.broadcasted_iota(jnp.int32, (span, 1, 1), 0)
    last = jnp.max(jnp.where(hit, turn[None], -1), axis=(1, 2))
    last = jnp.where(last < 0, spare, last)
    smem = pl.BlockSpec(memory_space=pltpu.SMEM)
    hbm = pl.BlockSpec(memory_space=pltpu.HBM)
    vmem = pl.BlockSpec(memory_space=pltpu.VMEM)
    sds = jax.ShapeDtypeStruct
    macs = blocks * cells * (4 * cells * ch * 7 + ch * ch * 12)
    hidden, flow, own, low, high = pl.pallas_call(
        functools.partial(main_kernel, n),
        out_shape=[
            sds((blocks, cells, ch), F32),
            sds((blocks, 2, cells), F32),
            sds((blocks, cells, ch), F32),
            sds((BW, cells, ch), BF16),
            sds((BW, cells, ch), BF16),
        ],
        in_specs=[smem] * 5 + [hbm] * 7 + [vmem] * 2,
        out_specs=[hbm, vmem, hbm, hbm, hbm],
        scratch_shapes=[
            pltpu.VMEM((span, cells, ch), BF16),
            pltpu.VMEM((BW, cells, ch), BF16),
            pltpu.VMEM((blocks, cells, ch), BF16),
            pltpu.VMEM((blocks, cells, ch), BF16),
            pltpu.VMEM((blocks, cells, ch), BF16),
            pltpu.VMEM(hid_weight.shape, BF16),
            pltpu.VMEM(in_weight.shape, BF16),
            pltpu.VMEM(cand_weight.shape, BF16),
            pltpu.VMEM((spare + 1, cells, ch), F32),
            pltpu.VMEM((blocks, cells, ch), F32),
            pltpu.VMEM((blocks, cells, ch), BF16),
            pltpu.VMEM((blocks, cells, cells), F32),
            pltpu.VMEM((blocks, cells, 2 * ch), F32),
            pltpu.VMEM((blocks, cells, ch), F32),
            pltpu.VMEM((2, BW, cells, ch), BF16),
            pltpu.SemaphoreType.DMA((7,)),
            pltpu.SemaphoreType.DMA((blocks // GROUP,)),
            pltpu.SemaphoreType.DMA((4,)),
            pltpu.SemaphoreType.DMA((4,)),
        ],
        compiler_params=pltpu.CompilerParams(
            vmem_limit_bytes=60 * 2**20, collective_id=0, has_side_effects=True
        ),
        cost_estimate=pl.CostEstimate(flops=2 * macs, bytes_accessed=10 * 2**20, transcendentals=0),
    )(
        listed, offsets, lengths, prev, last, first_feat, second_feat,
        hidden_init, cotangent, hid_weight, in_weight, cand_weight, disp_weight, gate_bias,
    )
    from_prev = jnp.where(me > 0, low.astype(F32), 0.0)
    from_next = jnp.where(me < n - 1, high.astype(F32), 0.0)
    own = jnp.concatenate(
        [own[:BW] + from_prev, own[BW : blocks - BW], own[blocks - BW :] + from_next], axis=0
    )
    return hidden, flow, own


def solution(mesh):
    lead = ("grp", "tile")
    return jax.shard_map(
        local,
        mesh=mesh,
        in_specs=(
            P(lead, None, None), P(lead, None, None), P(lead, None, None), P(lead, None, None),
            P(lead, None), P(None, lead), P(lead), P(), P(), P(), P(), P(),
        ),
        out_specs=(P(lead, None, None), P(lead, None, None), P(lead, None, None)),
        check_vma=False,
    )
```
